32 devices in a mesh: leaf: 32 (over z, y, x, core).
Axes of the slice: x: 2, y: 2, z: 4, core: 2. Of those that a mesh axis runs over, the one named last changes fastest.
Arguments:
- weights: float32 [131072, 128], P('leaf'), may hold values from -6 to 6
- labels: int32 [131072], P('leaf'), may hold values from 0 to 127
- basis: bfloat16 [512, 64, 256], P('leaf'), may hold values from -0.375 to 0.375
- near_tiles: bfloat16 [512, 3, 256, 256], P('leaf'), may hold values from -0.21875 to 0.21875
- near_ids: int32 [512, 2], P('leaf'), may hold values from 0 to 511, as said below
- transfer: bfloat16 [992, 64, 64], P('leaf'), may hold values from -0.5 to 0.5
- couplings: bfloat16 [992, 64, 256], P('leaf'), may hold values from -0.375 to 0.375
- sources: int32 [992, 4], P('leaf'), may hold values from 0 to 511, as said below
- coarse_transfer: bfloat16 [28, 64, 64], replicated, may hold values from -0.5 to 0.5
- coarse_couplings: bfloat16 [30, 64, 256], replicated, may hold values from -0.375 to 0.375
- coarse_sources: int32 [30, 4], replicated, may hold values from 0 to 15, as said below
Outputs:
- updated: float32 [131072, 128], P('leaf')
- second_scores: float32 [131072, 128], P('leaf')
The draws below stay inside these ranges and needn't reach their ends.
Inputs may be any that keep to these rules, and one draw needn't show every extreme that they name: `sources`: rows of device q's block name nodes of their row's level, numbered over all devices; the rows of one device name at most 4 nodes held by any single device (counted over all its rows), and some pair of devices reaches 4. `coarse_sources`: entries of a row name a node of that row's coarse level. `near_ids`: each entry lies within 2 leaves of its own leaf and differs from it; distance 2 occurs.
All inputs are finite; a program needn't handle non-finite values.
Results may differ from the reference program's by a relative error of at most 0.025.
Values may be sent and summed in bfloat16 or wider, within the bound.
No kernel may reach another device: no remote copies, remote signals or barrier semaphores. Data moves between devices by JAX's collectives and lax.ppermute only.
A program may use at most 128 MiB of HBM per device.

```python
import jax
import jax.numpy as jnp
import numpy as np

LEAF = 256
RANK = 64
CLASSES = 128
CPL = 4
REACH = 2
LEVELS = 5
LEAF_DEV = 16
NODES_DEV = 31
NLEAF = 512
POINTS = 131072
COARSE = 30
COARSE_MAPS = 28
CAP = 4
N_LEAF = 32


def draw_near_ids(key, part):
    leaves = jnp.arange(NLEAF, dtype=jnp.int32)
    lower = jax.random.randint(jax.random.fold_in(key, 11), (NLEAF,), 1, REACH + 1)
    upper = jax.random.randint(jax.random.fold_in(key, 12), (NLEAF,), 1, REACH + 1)
    lower = jnp.where(leaves % 5 == 2, REACH, lower)
    upper = jnp.where(leaves % 7 == 3, REACH, upper)
    below = jnp.where(leaves - lower >= 0, leaves - lower, leaves + lower)
    above = jnp.where(leaves + upper < NLEAF, leaves + upper, leaves - upper)
    return jnp.stack([below, above], axis=1).astype(jnp.int32)


def draw_sources(key, part):
    row_height = np.concatenate([np.full(LEAF_DEV >> height, height) for height in range(LEVELS)])
    slot_count = jnp.asarray(np.repeat(LEAF_DEV >> row_height, CPL), dtype=jnp.int32)
    slot_total = NODES_DEV * CPL

    def per_device(device):
        subkey = jax.random.fold_in(key, device)
        shuffled = jax.random.permutation(jax.random.fold_in(subkey, 1), N_LEAF * CAP)[:slot_total]
        owner_dev = (shuffled // CAP).astype(jnp.int32)
        raw = jax.random.randint(jax.random.fold_in(subkey, 2), (slot_total,), 0, 1 << 30)
        within = raw % slot_count
        return (owner_dev * slot_count + within).reshape(NODES_DEV, CPL)
    listing = jax.vmap(per_device)(jnp.arange(N_LEAF, dtype=jnp.int32))
    return listing.reshape(N_LEAF * NODES_DEV, CPL).astype(jnp.int32)


def draw_coarse_sources(key, part):
    height_top = int(N_LEAF).bit_length() - 2
    level_sizes = np.concatenate([np.full(N_LEAF >> height, N_LEAF >> height) for height in range(1, height_top + 1)])
    raw = jax.random.randint(key, (N_LEAF - 2, CPL), 0, 1 << 30)
    return (raw % jnp.asarray(level_sizes, dtype=jnp.int32)[:, None]).astype(jnp.int32)


def set_ends(drawn, key, least, largest):
    place = [jax.random.randint(jax.random.fold_in(key, axis), (), 0, length) for axis, length in enumerate(drawn.shape)]
    longest = drawn.shape.index(max(drawn.shape))
    next_to = place[:longest] + [(place[longest] + 1) % drawn.shape[longest]] + place[longest + 1:]
    return drawn.at[tuple(place)].set(least).at[tuple(next_to)].set(largest)


def block_levels(key, shape, shards, least, largest):
    def one(dim, parts):
        heights = jax.random.uniform(jax.random.fold_in(jax.random.fold_in(key, 6), dim), (parts,), jnp.float32, least / len(shards), largest / len(shards))
        return jnp.repeat(jnp.exp(heights), shape[dim] // parts).reshape((-1,) + (1,) * (len(shape) - dim - 1))

    factor_of = one(*shards[0])
    for cut in shards[1:]:
        factor_of = factor_of * one(*cut)
    return factor_of


def bell_draw(own_key, shape, scale, reach, pieces=(), held_as=jnp.bfloat16):
    level = block_levels(own_key, shape, pieces, -0.22, 0.18) if pieces else 1.0
    entries = jax.random.normal(own_key, shape, jnp.float32) * scale * level
    return jnp.minimum(jnp.maximum(entries, -reach), reach).astype(held_as)


def setup_inputs(seed: int = 0) -> dict:
    keys = jax.random.split(jax.random.key(seed), 12)
    weights = bell_draw(keys[0], (POINTS, CLASSES), 1.0, 6.0, ((0, 32),), jnp.float32)
    labels = set_ends(jax.random.randint(keys[1], (POINTS,), 0, CLASSES), jax.random.fold_in(keys[1], 1), 0, CLASSES - 1).astype(jnp.int32)
    basis = bell_draw(keys[2], (NLEAF, RANK, LEAF), LEAF ** -0.5, 0.375, ((0, 32),))
    near_tiles = bell_draw(keys[3], (NLEAF, 3, LEAF, LEAF), (3 * LEAF) ** -0.5, 0.21875, ((0, 32),))
    near_ids = draw_near_ids(jax.random.fold_in(keys[11], 71), 0)
    transfer = bell_draw(keys[5], (N_LEAF * NODES_DEV, RANK, RANK), (2 * RANK) ** -0.5, 0.5, ((0, 32),))
    couplings = bell_draw(keys[6], (N_LEAF * NODES_DEV, RANK, CPL * RANK), (CPL * RANK) ** -0.5, 0.375, ((0, 32),))
    sources = draw_sources(jax.random.fold_in(keys[11], 71), 0)
    coarse_transfer = bell_draw(keys[8], (COARSE_MAPS, RANK, RANK), (2 * RANK) ** -0.5, 0.5)
    coarse_couplings = bell_draw(keys[9], (COARSE, RANK, CPL * RANK), (CPL * RANK) ** -0.5, 0.375)
    coarse_sources = draw_coarse_sources(jax.random.fold_in(keys[11], 71), 0)
    return {"weights": weights, "labels": labels, "basis": basis, "near_tiles": near_tiles, "near_ids": near_ids, "transfer": transfer, "couplings": couplings, "sources": sources, "coarse_transfer": coarse_transfer, "coarse_couplings": coarse_couplings, "coarse_sources": coarse_sources}


step_size = 0.5


def coupling_term(level_coef, mats, lists):
    blocks = level_coef[lists].astype(jnp.float32)
    blocks = blocks.reshape(lists.shape[0], lists.shape[1] * level_coef.shape[1], level_coef.shape[2])
    return jnp.einsum("tab,tbn->tan", mats.astype(jnp.float32), blocks)


def upward(children, mats):
    half = children.shape[0] // 2
    joined = mats.astype(jnp.float32).reshape(half, 2, mats.shape[1], mats.shape[2])
    kids = children.astype(jnp.float32).reshape(half, 2, children.shape[1], children.shape[2])
    return jnp.einsum("jkcp,jkcn->jpn", joined, kids).astype(jnp.bfloat16)


def downward(coupled, mats, parent_field):
    half = parent_field.shape[0]
    joined = mats.astype(jnp.float32).reshape(half, 2, mats.shape[1], mats.shape[2])
    pushed = jnp.einsum("jkcp,jpn->jkcn", joined, parent_field.astype(jnp.float32))
    return (coupled + pushed.reshape(coupled.shape)).astype(jnp.bfloat16)


def operate(point_vals, basis, near_tiles, near_ids, transfer, couplings, sources, coarse_transfer, coarse_couplings, coarse_sources):
    devices = N_LEAF
    node_count = NODES_DEV
    counts = [LEAF_DEV >> height for height in range(LEVELS)]
    starts = [sum(counts[:height]) for height in range(LEVELS)]
    point_rows = point_vals.reshape(NLEAF, LEAF, CLASSES)
    leaf_coef = jnp.einsum("trp,tpn->trn", basis.astype(jnp.float32), point_rows.astype(jnp.float32)).astype(jnp.bfloat16)
    maps_dev = transfer.reshape(devices, node_count, RANK, RANK)
    mats_dev = couplings.reshape(devices, node_count, RANK, CPL * RANK)
    lists_dev = sources.reshape(devices, node_count, CPL)

    def level_rows(array, height):
        part_rows = array[:, starts[height]:starts[height] + counts[height]]
        return part_rows.reshape((devices * counts[height],) + array.shape[2:])

    coefs = [leaf_coef]
    for height in range(LEVELS - 1):
        coefs.append(upward(coefs[-1], level_rows(maps_dev, height)))
    coarse = [coefs[-1]]
    coarse.append(upward(coarse[-1], maps_dev[:, node_count - 1]))
    coarse_levels = devices.bit_length() - 2
    for height in range(1, coarse_levels):
        offset = devices - (devices >> (height - 1))
        level_count = devices >> height
        coarse.append(upward(coarse[-1], coarse_transfer[offset:offset + level_count]))
    node_field = None
    for height in range(coarse_levels, 0, -1):
        offset = devices - (devices >> (height - 1))
        level_count = devices >> height
        coupled = coupling_term(coarse[height], coarse_couplings[offset:offset + level_count], coarse_sources[offset:offset + level_count])
        if height == coarse_levels:
            node_field = coupled.astype(jnp.bfloat16)
        else:
            node_field = downward(coupled, coarse_transfer[offset:offset + level_count], node_field)
    for height in range(LEVELS - 1, -1, -1):
        coupled = coupling_term(coefs[height], level_rows(mats_dev, height), level_rows(lists_dev, height))
        if height == LEVELS - 1:
            mats = maps_dev[:, node_count - 1]
        else:
            mats = level_rows(maps_dev, height)
        node_field = downward(coupled, mats, node_field)
    near_term = jnp.einsum("trp,trn->tpn", basis.astype(jnp.float32), node_field.astype(jnp.float32))
    neighbours = [point_rows, point_rows[near_ids[:, 0]], point_rows[near_ids[:, 1]]]
    for member in range(3):
        near_term = near_term + jnp.einsum("tpq,tqn->tpn", near_tiles[:, member].astype(jnp.float32), neighbours[member].astype(jnp.float32))
    return near_term.reshape(POINTS, CLASSES)


def reference(weights, labels, basis, near_tiles, near_ids, transfer, couplings, sources, coarse_transfer, coarse_couplings, coarse_sources):
    onehot = (labels[:, None] == jnp.arange(CLASSES, dtype=jnp.int32)[None, :]).astype(jnp.float32)
    extra = (basis, near_tiles, near_ids, transfer, couplings, sources, coarse_transfer, coarse_couplings, coarse_sources)
    first_scores = operate(weights.astype(jnp.bfloat16), *extra)
    middle = weights - step_size * (jax.nn.sigmoid(first_scores) - onehot)
    second_scores = operate(middle.astype(jnp.bfloat16), *extra)
    updated = middle - step_size * (jax.nn.sigmoid(second_scores) - onehot)
    return (updated, second_scores)
```

```python
import functools

import jax
import jax.numpy as jnp
import numpy as np
from jax import lax
from jax.experimental import pallas as pl
from jax.experimental.pallas import tpu as pltpu
from jax.sharding import PartitionSpec as P

REACH = 2
STEP_SIZE = 0.5
MIB = 1 << 20
F32 = jnp.float32
BF16 = jnp.bfloat16


def rows_dot(left, right):
    return lax.dot_general(left, right, (((0,), (0,)), ((), ())), preferred_element_type=F32)


def dot(left, right):
    return jnp.dot(left, right, preferred_element_type=F32)


def pair_rows(ref, first):
    both = ref[pl.ds(first, 2)]
    return both.reshape(2 * both.shape[1], both.shape[2])


def tree_rows(per_dev):
    counts = [per_dev >> height for height in range(per_dev.bit_length())]
    starts = [sum(counts[:height]) for height in range(len(counts))]
    return counts, starts


def go_up(coef, transfer, per_dev):
    counts, starts = tree_rows(per_dev)
    for height in range(1, len(counts)):
        for node in range(counts[height]):
            kids = starts[height - 1] + 2 * node
            coef[starts[height] + node] = rows_dot(
                pair_rows(transfer, kids), pair_rows(coef, kids)
            ).astype(BF16)


def go_down(field, coupled, transfer, parent, per_dev):
    counts, starts = tree_rows(per_dev)
    top = starts[-1]
    field[top] = (coupled[top] + dot(transfer[top], parent)).astype(BF16)
    for height in range(len(counts) - 2, -1, -1):
        for node in range(counts[height + 1]):
            kids = starts[height] + 2 * node
            pushed = dot(pair_rows(transfer, kids), field[starts[height + 1] + node])
            both = pair_rows(coupled, kids) + pushed
            field[pl.ds(kids, 2)] = both.reshape(2, -1, both.shape[1]).astype(BF16)


def first_kernel(per_dev, weights, basis, transfer, values, coef, top_part):
    step = pl.program_id(0)
    block = basis.shape[0]
    for leaf in range(block):
        rounded = weights[leaf].astype(BF16)
        values[leaf] = rounded
        coef[step * block + leaf] = dot(basis[leaf], rounded).astype(BF16)

    @pl.when(step == pl.num_programs(0) - 1)
    def _():
        go_up(coef, transfer, per_dev)
        top = coef.shape[0] - 1
        top_part[...] = rows_dot(transfer[top], coef[top])


def pick_kernel(chosen, coef, payload):
    for slot in range(payload.shape[0]):
        payload[slot] = coef[chosen[slot]]


def near_kernel(ids, before, own, after, tiles, out, padded):
    step = pl.program_id(0)
    block = tiles.shape[0]
    reach = before.shape[0]
    inner = own.shape[0]

    @pl.when(step == 0)
    def _():
        padded[pl.ds(0, reach)] = before[...]
        padded[pl.ds(reach, inner)] = own[...]
        padded[pl.ds(reach + inner, reach)] = after[...]

    for leaf in range(block):
        row = step * block + leaf
        out[leaf] = (
            dot(tiles[leaf, 0], padded[row + reach])
            + dot(tiles[leaf, 1], padded[ids[2 * row]])
            + dot(tiles[leaf, 2], padded[ids[2 * row + 1]])
        )


def coarse_kernel(devices, me, listed, gathered, transfer, couplings, out, coef):
    levels = devices.bit_length() - 2
    links = couplings.shape[2] // couplings.shape[1]
    offsets = [devices - (devices >> level - 1) for level in range(1, levels + 1)]
    mine = me[0]
    for node in range(devices // 2):
        coef[node] = gathered[jnp.bitwise_xor(mine >> 1, node)]
    for level in range(1, levels):
        for node in range(devices >> level + 1):
            kids = offsets[level - 1] + 2 * node
            coef[offsets[level] + node] = rows_dot(
                pair_rows(transfer, kids), pair_rows(coef, kids)
            ).astype(BF16)
    field = None
    for level in range(levels, 0, -1):
        offset = offsets[level - 1]
        node = offset + (mine >> level)
        blocks = jnp.concatenate(
            [coef[offset + listed[node * links + link]] for link in range(links)], axis=0
        )
        term = dot(couplings[node], blocks)
        if level < levels:
            term = term + dot(transfer[node], field)
        field = term.astype(BF16)
    out[...] = field


def finish_kernel(
    per_dev, last, landing, chosen, incoming, couplings, transfer, parent, near, base, basis, *rest
):
    if last:
        scores_out, new_out, field, coupled = rest
    else:
        new_out, values, payload, top_part, field, coupled, coef = rest
    step = pl.program_id(0)
    block = basis.shape[0]
    links = couplings.shape[2] // couplings.shape[1]

    @pl.when(step == 0)
    def _():
        for node in range(couplings.shape[0]):
            blocks = jnp.concatenate(
                [incoming[landing[node * links + link]] for link in range(links)], axis=0
            )
            coupled[node] = dot(couplings[node], blocks)
        go_down(field, coupled, transfer, parent[...], per_dev)

    for leaf in range(block):
        row = step * block + leaf
        scores = near[leaf] + rows_dot(basis[leaf], field[row])
        new = base[leaf] - (0.5 * STEP_SIZE) * (1.0 + jnp.tanh(0.5 * scores))
        new_out[leaf] = new
        if last:
            scores_out[leaf] = scores
        else:
            rounded = new.astype(BF16)
            values[leaf] = rounded
            coef[row] = dot(basis[leaf], rounded).astype(BF16)

    if not last:

        @pl.when(step == pl.num_programs(0) - 1)
        def _():
            go_up(coef, transfer, per_dev)
            top = coef.shape[0] - 1
            top_part[...] = rows_dot(transfer[top], coef[top])
            for slot in range(payload.shape[0]):
                payload[slot] = coef[chosen[slot]]


def whole(shape):
    return pl.BlockSpec(shape, lambda i, *_: (0,) * len(shape), pipeline_mode=pl.Buffered(1))


def whole_out(shape):
    return pl.BlockSpec(shape, lambda i, *_: (0,) * len(shape))


def per_step(block, shape):
    return pl.BlockSpec((block,) + tuple(shape[1:]), lambda i, *_: (i,) + (0,) * (len(shape) - 1))


def params(limit):
    return pltpu.CompilerParams(
        dimension_semantics=("arbitrary",), vmem_limit_bytes=limit * MIB
    )


def cost(flops, moved):
    return pl.CostEstimate(flops=int(flops), bytes_accessed=int(moved), transcendentals=0)


def plan(sources, devices, per_dev, capacity):
    counts, starts = tree_rows(per_dev)
    links = sources.shape[1]
    heights = np.repeat(np.arange(len(counts)), np.array(counts) * links)
    shift = jnp.asarray((len(counts) - 1 - heights).astype(np.int32))
    start = jnp.asarray(np.array(starts)[heights].astype(np.int32))
    mask = jnp.asarray((np.array(counts)[heights] - 1).astype(np.int32))
    flat = sources.reshape(-1)
    owner = flat >> shift
    row = start + (flat & mask)
    width = flat.shape[0]
    earlier = jnp.asarray(np.tril(np.ones((width, width), dtype=bool), -1))
    rank = jnp.sum(((owner[:, None] == owner[None, :]) & earlier).astype(jnp.int32), axis=1)
    landing = owner * capacity + rank
    slots = jnp.arange(devices * capacity, dtype=jnp.int32)
    wanted = jnp.sum(jnp.where(landing[None, :] == slots[:, None], row[None, :], 0), axis=1)
    chosen = lax.all_to_all(
        wanted.reshape(devices, capacity), "leaf", split_axis=0, concat_axis=0, tiled=True
    )
    return landing, chosen.reshape(-1)


def local(
    weights,
    labels,
    basis,
    near_tiles,
    near_ids,
    transfer,
    couplings,
    sources,
    coarse_transfer,
    coarse_couplings,
    coarse_sources,
):
    devices = lax.axis_size("leaf")
    me = lax.axis_index("leaf")
    per_dev, rank_dim, leaf_size = basis.shape
    classes = weights.shape[1]
    nodes = transfer.shape[0]
    links = sources.shape[1]
    capacity = nodes * links // devices + 1
    slots = devices * capacity
    block = next(size for size in (4, 2, 1) if per_dev % size == 0)
    steps = per_dev // block
    node_shape = (rank_dim, classes)
    leaf_shape = (per_dev, leaf_size, classes)
    weights3 = weights.reshape(leaf_shape)
    offset_ids = (near_ids - (me * per_dev - REACH)).reshape(-1)

    landing, chosen = plan(sources, devices, per_dev, capacity)

    values, coef, top_part = pl.pallas_call(
        functools.partial(first_kernel, per_dev),
        grid=(steps,),
        in_specs=[
            per_step(block, leaf_shape),
            per_step(block, basis.shape),
            whole(transfer.shape),
        ],
        out_specs=[
            per_step(block, leaf_shape),
            whole_out((nodes,) + node_shape),
            whole_out(node_shape),
        ],
        out_shape=[
            jax.ShapeDtypeStruct(leaf_shape, BF16),
            jax.ShapeDtypeStruct((nodes,) + node_shape, BF16),
            jax.ShapeDtypeStruct(node_shape, F32),
        ],
        compiler_params=params(16),
        cost_estimate=cost(2 * basis.size * classes, 4 * weights.size),
        name="leaf_coefs",
    )(weights3, basis, transfer)

    payload = pl.pallas_call(
        pick_kernel,
        grid=(1,),
        in_specs=[
            pl.BlockSpec(memory_space=pltpu.SMEM),
            whole((nodes,) + node_shape),
        ],
        out_specs=whole_out((slots,) + node_shape),
        out_shape=jax.ShapeDtypeStruct((slots,) + node_shape, BF16),
        compiler_params=params(16),
        cost_estimate=cost(0, 4 * slots * rank_dim * classes),
        name="pick_rows",
    )(chosen, coef)

    def exchange(payload):
        return lax.all_to_all(payload, "leaf", split_axis=0, concat_axis=0, tiled=True)

    def near_field(values):
        up = [(i, i + 1) for i in range(devices - 1)]
        down = [(j, i) for i, j in up]
        before = lax.ppermute(values[per_dev - REACH :], "leaf", up)
        after = lax.ppermute(values[:REACH], "leaf", down)
        halo = (REACH, leaf_size, classes)
        return pl.pallas_call(
            near_kernel,
            grid=(steps,),
            in_specs=[
                pl.BlockSpec(memory_space=pltpu.SMEM),
                whole(halo),
                whole(leaf_shape),
                whole(halo),
                per_step(block, near_tiles.shape),
            ],
            out_specs=per_step(block, leaf_shape),
            out_shape=jax.ShapeDtypeStruct(leaf_shape, F32),
            scratch_shapes=[pltpu.VMEM((per_dev + 2 * REACH, leaf_size, classes), BF16)],
            compiler_params=params(24),
            cost_estimate=cost(2 * near_tiles.size * classes, 2 * near_tiles.size),
            name="near_field",
        )(offset_ids, before, values, after, near_tiles)

    def coarse_field(top_part):
        other = lax.ppermute(top_part, "leaf", [(i, i ^ 1) for i in range(devices)])
        gathered = (top_part + other).astype(BF16)[None]
        hop = 2
        while hop < devices:
            arrived = lax.ppermute(gathered, "leaf", [(i, i ^ hop) for i in range(devices)])
            gathered = jnp.concatenate([gathered, arrived], axis=0)
            hop *= 2
        smem = pl.BlockSpec(memory_space=pltpu.SMEM)
        return pl.pallas_call(
            functools.partial(coarse_kernel, devices),
            grid=(1,),
            in_specs=[
                smem,
                smem,
                whole(gathered.shape),
                whole(coarse_transfer.shape),
                whole(coarse_couplings.shape),
            ],
            out_specs=whole_out(node_shape),
            out_shape=jax.ShapeDtypeStruct(node_shape, BF16),
            scratch_shapes=[pltpu.VMEM((coarse_couplings.shape[0],) + node_shape, BF16)],
            compiler_params=params(16),
            cost_estimate=cost(2 * coarse_couplings.size * classes, 2 * coarse_couplings.size),
            name="coarse_field",
        )(
            me.reshape(1),
            coarse_sources.reshape(-1),
            gathered,
            coarse_transfer,
            coarse_couplings,
        )

    def finish(incoming, parent, near, base, last):
        leaf_out = jax.ShapeDtypeStruct(leaf_shape, F32)
        scratch = [
            pltpu.VMEM((nodes,) + node_shape, BF16),
            pltpu.VMEM((nodes,) + node_shape, F32),
        ]
        if last:
            out_shape = [leaf_out, leaf_out]
            out_specs = [per_step(block, leaf_shape)] * 2
        else:
            out_shape = [
                leaf_out,
                jax.ShapeDtypeStruct(leaf_shape, BF16),
                jax.ShapeDtypeStruct((slots,) + node_shape, BF16),
                jax.ShapeDtypeStruct(node_shape, F32),
            ]
            out_specs = [
                per_step(block, leaf_shape),
                per_step(block, leaf_shape),
                whole_out((slots,) + node_shape),
                whole_out(node_shape),
            ]
            scratch.append(pltpu.VMEM((nodes,) + node_shape, BF16))
        return pl.pallas_call(
            functools.partial(finish_kernel, per_dev, last),
            grid_spec=pltpu.PrefetchScalarGridSpec(
                num_scalar_prefetch=2,
                grid=(steps,),
                in_specs=[
                    whole(incoming.shape),
                    whole(couplings.shape),
                    whole(transfer.shape),
                    whole(node_shape),
                    per_step(block, leaf_shape),
                    per_step(block, leaf_shape),
                    per_step(block, basis.shape),
                ],
                out_specs=out_specs,
                scratch_shapes=scratch,
            ),
            out_shape=out_shape,
            compiler_params=params(32),
            cost_estimate=cost(2 * couplings.size * classes, 12 * weights.size),
            name="last_scores" if last else "first_scores",
        )(landing, chosen, incoming, couplings, transfer, parent, near, base, basis)

    shift_up = STEP_SIZE * (
        labels[:, None] == jnp.arange(classes, dtype=jnp.int32)[None, :]
    ).astype(F32).reshape(leaf_shape)

    incoming = exchange(payload)
    near = near_field(values)
    parent = coarse_field(top_part)
    middle, values, payload, top_part = finish(
        incoming, parent, near, weights3 + shift_up, False
    )
    incoming = exchange(payload)
    near = near_field(values)
    parent = coarse_field(top_part)
    second_scores, updated = finish(incoming, parent, near, middle + shift_up, True)
    return updated.reshape(weights.shape), second_scores.reshape(weights.shape)


def solution(mesh):
    in_specs = (
        P("leaf", None),
        P("leaf"),
        P("leaf", None, None),
        P("leaf", None, None, None),
        P("leaf", None),
        P("leaf", None, None),
        P("leaf", None, None),
        P("leaf", None),
        P(),
        P(),
        P(),
    )
    out_specs = (P("leaf", None), P("leaf", None))
    return jax.shard_map(local, mesh=mesh, in_specs=in_specs, out_specs=out_specs, check_vma=False)
```

```python
import functools

import jax
import jax.numpy as jnp
import numpy as np
from jax import lax
from jax.experimental import pallas as pl
from jax.experimental.pallas import tpu as pltpu
from jax.sharding import PartitionSpec as P

REACH = 2
STEP_SIZE = 0.5
MIB = 1 << 20
F32 = jnp.float32
BF16 = jnp.bfloat16


def rows_dot(left, right):
    return lax.dot_general(left, right, (((0,), (0,)), ((), ())), preferred_element_type=F32)


def dot(left, right):
    return jnp.dot(left, right, preferred_element_type=F32)


def pair_rows(ref, first):
    both = ref[pl.ds(first, 2)]
    return both.reshape(2 * both.shape[1], both.shape[2])


def tree_rows(per_dev):
    counts = [per_dev >> height for height in range(per_dev.bit_length())]
    starts = [sum(counts[:height]) for height in range(len(counts))]
    return counts, starts


def go_up(coef, transfer, per_dev):
    counts, starts = tree_rows(per_dev)
    for height in range(1, len(counts)):
        for node in range(counts[height]):
            kids = starts[height - 1] + 2 * node
            coef[starts[height] + node] = rows_dot(
                pair_rows(transfer, kids), pair_rows(coef, kids)
            ).astype(BF16)


def go_down(field, coupled, transfer, parent, per_dev):
    counts, starts = tree_rows(per_dev)
    top = starts[-1]
    field[top] = (coupled[top] + dot(transfer[top], parent)).astype(BF16)
    for height in range(len(counts) - 2, -1, -1):
        for node in range(counts[height + 1]):
            kids = starts[height] + 2 * node
            pushed = dot(pair_rows(transfer, kids), field[starts[height + 1] + node])
            both = pair_rows(coupled, kids) + pushed
            field[pl.ds(kids, 2)] = both.reshape(2, -1, both.shape[1]).astype(BF16)


def chunks(total, size):
    return [(low, min(size, total - low)) for low in range(0, total, size)]


class Mover:
    def __init__(self, sems):
        self.sems = sems
        self.used = 0

    def start(self, source, target):
        copy = pltpu.make_async_copy(source, target, self.sems.at[self.used])
        self.used += 1
        copy.start()
        return copy


LEAVES = 8


def first_kernel(per_dev, weights, basis, transfer, coef, top_part, wbuf, bbuf, tbuf, sems):
    mover = Mover(sems)
    parts = chunks(per_dev, LEAVES)
    basis_in = mover.start(basis, bbuf)
    arriving = [mover.start(weights.at[pl.ds(*part)], wbuf.at[pl.ds(*part)]) for part in parts]
    transfer_in = mover.start(transfer, tbuf)
    basis_in.wait()
    for (low, size), copy in zip(parts, arriving):
        copy.wait()
        for leaf in range(low, low + size):
            coef[leaf] = dot(bbuf[leaf], wbuf[leaf].astype(BF16)).astype(BF16)
    transfer_in.wait()
    go_up(coef, tbuf, per_dev)
    top = coef.shape[0] - 1
    top_part[...] = rows_dot(tbuf[top], coef[top])


def pick(mover, chosen, coef, buffer, payload):
    leaving = []
    total, width = payload.shape[0], chosen.shape[2]
    for low, size in chunks(total, max(total // 2, 1)):
        for slot in range(low, low + size):
            buffer[slot] = coef[chosen[slot // width, 0, slot % width]]
        rows = pl.ds(low, size)
        leaving.append(mover.start(buffer.at[rows], payload.at[rows]))
    return leaving


def pick_kernel(chosen, coef, payload, buffer, sems):
    for copy in pick(Mover(sems), chosen, coef, buffer, payload):
        copy.wait()


def near_kernel(ids, own, tiles, out, padded):
    step = pl.program_id(0)
    block = tiles.shape[0]
    inner = own.shape[0]

    @pl.when(step == 0)
    def _():
        nothing = jnp.zeros((REACH,) + own.shape[1:], BF16)
        padded[pl.ds(0, REACH)] = nothing
        padded[pl.ds(REACH, inner)] = own[...]
        padded[pl.ds(REACH + inner, REACH)] = nothing

    for leaf in range(block):
        row = step * block + leaf
        out[leaf] = (
            dot(tiles[leaf, 0], padded[row + REACH])
            + dot(tiles[leaf, 1], padded[ids[2 * row]])
            + dot(tiles[leaf, 2], padded[ids[2 * row + 1]])
        )


def join_kernel(first, second, *rest):
    joined = rest[-1]
    size = first.shape[0]
    joined[pl.ds(0, size)] = first[...]
    joined[pl.ds(size, size)] = second[...]


def edge_scores(ids, leaf, tiles, halo, per_dev):
    total = None
    for member in range(2):
        row = ids[2 * leaf + member]
        place = jnp.where(row < REACH, row, jnp.where(row < REACH + per_dev, 2 * REACH, row - per_dev))
        term = dot(tiles[member], halo[place])
        total = term if total is None else total + term
    return total


def coarse_parent(devices, order, mine, listed, halves, transfer, couplings, coef):
    levels = devices.bit_length() - 2
    links = couplings.shape[2] // couplings.shape[1]
    offsets = [devices - (devices >> level - 1) for level in range(1, levels + 1)]
    depth = halves[0].shape[1]
    for turn, half in enumerate(halves):
        rows = pl.ds(pl.multiple_of(jnp.bitwise_xor(mine & 1, turn) * depth, depth), depth)
        for place in range(devices // 2):
            coef[jnp.bitwise_xor(mine >> 1, order[place]), rows] = half[place]
    for level in range(1, levels):
        for node in range(devices >> level + 1):
            kids = offsets[level - 1] + 2 * node
            coef[offsets[level] + node] = rows_dot(
                pair_rows(transfer, kids), pair_rows(coef, kids)
            ).astype(BF16)
    field = None
    for level in range(levels, 0, -1):
        offset = offsets[level - 1]
        node = offset + (mine >> level)
        blocks = jnp.concatenate(
            [coef[offset + listed[node * links + link]] for link in range(links)], axis=0
        )
        term = dot(couplings[level - 1], blocks)
        if level < levels:
            term = term + dot(transfer[node], field)
        field = term.astype(BF16)
    return field


def finish_kernel(
    devices,
    order,
    per_dev,
    last,
    me,
    listed,
    landing,
    chosen,
    ids,
    incoming,
    couplings,
    transfer,
    half,
    other_half,
    coarse_transfer,
    coarse_couplings,
    near,
    base,
    basis,
    before,
    after,
    tiles,
    *rest,
):
    if last:
        new_out, scores_out = rest[:2]
        rest = rest[2:]
    else:
        payload, new_out, values_out, top_part = rest[:4]
        rest = rest[4:]
        coef, buffer, values = rest[-4:-1]
    inbuf, cbuf, tbuf, nbuf, abuf, bbuf, halo, edge_tiles, field, coupled = rest[:10]
    coarse_maps, coarse_mats, coarse_coef = rest[10:13]
    sems = rest[-1]
    mine = me[0]
    nodes = couplings.shape[0]
    links = couplings.shape[2] // couplings.shape[1]
    mover = Mover(sems)
    low_edge, high_edge = pl.ds(0, REACH), pl.ds(per_dev - REACH, REACH)
    others = pl.ds(1, 2)
    coarse_in = [mover.start(coarse_transfer, coarse_maps)]
    for level in range(1, coarse_mats.shape[0] + 1):
        node = devices - (devices >> level - 1) + (mine >> level)
        coarse_in.append(mover.start(coarse_couplings.at[node], coarse_mats.at[level - 1]))
    blocks_in, mats_in, maps_in, *leaves_in = [
        mover.start(*pair)
        for pair in (
            (incoming, inbuf),
            (couplings, cbuf),
            (transfer, tbuf),
            (before, halo.at[pl.ds(0, REACH)]),
            (after, halo.at[pl.ds(REACH, REACH)]),
            (tiles.at[low_edge, others], edge_tiles.at[pl.ds(0, REACH)]),
            (tiles.at[high_edge, others], edge_tiles.at[pl.ds(REACH, REACH)]),
            (basis, bbuf),
            (near, nbuf),
            (base, abuf),
        )
    ]
    halo[2 * REACH] = jnp.zeros(halo.shape[1:], BF16)
    for copy in coarse_in:
        copy.wait()
    parent = coarse_parent(
        devices, order, mine, listed, (half, other_half), coarse_maps, coarse_mats, coarse_coef
    )
    blocks_in.wait()
    mats_in.wait()
    for node in range(nodes - 1, -1, -1):
        blocks = jnp.concatenate(
            [inbuf[landing[node * links + link]] for link in range(links)], axis=0
        )
        coupled[node] = dot(cbuf[node], blocks)
    maps_in.wait()
    go_down(field, coupled, tbuf, parent, per_dev)
    leaving = []
    for copy in leaves_in:
        copy.wait()
    for low, size in chunks(per_dev, LEAVES):
        rows = pl.ds(low, size)
        for leaf in range(low, low + size):
            scores = nbuf[leaf] + rows_dot(bbuf[leaf], field[leaf])
            edge = leaf if leaf < REACH else leaf - (per_dev - 2 * REACH)
            if leaf < REACH or leaf >= per_dev - REACH:
                scores = scores + edge_scores(ids, leaf, edge_tiles.at[edge], halo, per_dev)
            new = abuf[leaf] - gradient(scores)
            abuf[leaf] = new
            if last:
                nbuf[leaf] = scores
            else:
                rounded = new.astype(BF16)
                values[leaf] = rounded
                coef[leaf] = dot(bbuf[leaf], rounded).astype(BF16)
        if last:
            leaving.append(mover.start(nbuf.at[rows], scores_out.at[rows]))
        else:
            leaving.append(mover.start(values.at[rows], values_out.at[rows]))
        leaving.append(mover.start(abuf.at[rows], new_out.at[rows]))
    if not last:
        go_up(coef, tbuf, per_dev)
        leaving += pick(mover, chosen, coef, buffer, payload)
        top_part[...] = rows_dot(tbuf[nodes - 1], coef[nodes - 1])
    for copy in leaving:
        copy.wait()


def gradient(scores):
    return (0.5 * STEP_SIZE) * (1.0 + jnp.tanh(0.5 * scores))


def shifted(new, labels, classes):
    marks = lax.broadcasted_iota(jnp.int32, (classes, labels.shape[1]), 0) == labels
    eye = lax.broadcasted_iota(jnp.int32, (classes, classes), 0) == lax.broadcasted_iota(
        jnp.int32, (classes, classes), 1
    )
    return new + STEP_SIZE * rows_dot(marks.astype(BF16), eye.astype(BF16))


def shift_kernel(new, labels, base):
    for leaf in range(new.shape[0]):
        base[leaf] = shifted(new[leaf], labels[leaf], new.shape[2])


def whole(shape):
    return pl.BlockSpec(shape, lambda i, *_: (0,) * len(shape), pipeline_mode=pl.Buffered(1))


def whole_out(shape):
    return pl.BlockSpec(shape, lambda i, *_: (0,) * len(shape))


def per_step(block, shape):
    return pl.BlockSpec((block,) + tuple(shape[1:]), lambda i, *_: (i,) + (0,) * (len(shape) - 1))


def params(limit):
    return pltpu.CompilerParams(
        dimension_semantics=("arbitrary",), vmem_limit_bytes=limit * MIB
    )


def cost(flops, moved):
    return pl.CostEstimate(flops=int(flops), bytes_accessed=int(moved), transcendentals=0)


def plan(sources, devices, per_dev, capacity):
    counts, starts = tree_rows(per_dev)
    links = sources.shape[1]
    heights = np.repeat(np.arange(len(counts)), np.array(counts) * links)
    shift = jnp.asarray((len(counts) - 1 - heights).astype(np.int32))
    start = jnp.asarray(np.array(starts)[heights].astype(np.int32))
    mask = jnp.asarray((np.array(counts)[heights] - 1).astype(np.int32))
    flat = sources.reshape(-1)
    owner = flat >> shift
    row = start + (flat & mask)
    width = flat.shape[0]
    earlier = jnp.asarray(np.tril(np.ones((width, width), dtype=bool), -1))
    rank = jnp.sum(((owner[:, None] == owner[None, :]) & earlier).astype(jnp.int32), axis=1)
    landing = owner * capacity + rank
    slots = jnp.arange(devices * capacity, dtype=jnp.int32)
    wanted = jnp.sum(jnp.where(landing[None, :] == slots[:, None], row[None, :], 0), axis=1)
    chosen = lax.all_to_all(
        wanted.reshape(devices, 1, capacity), "leaf", split_axis=0, concat_axis=0, tiled=True
    )
    return landing, chosen


def local(
    weights,
    labels,
    basis,
    near_tiles,
    near_ids,
    transfer,
    couplings,
    sources,
    coarse_transfer,
    coarse_couplings,
    coarse_sources,
):
    devices = lax.axis_size("leaf")
    me = lax.axis_index("leaf")
    per_dev, rank_dim, leaf_size = basis.shape
    classes = weights.shape[1]
    nodes = transfer.shape[0]
    links = sources.shape[1]
    capacity = nodes * links // devices + 1
    slots = devices * capacity
    block = next(size for size in (4, 2, 1) if per_dev % size == 0)
    steps = per_dev // block
    node_shape = (rank_dim, classes)
    leaf_shape = (per_dev, leaf_size, classes)
    weights3 = weights.reshape(leaf_shape)
    offset_ids = (near_ids - (me * per_dev - REACH)).reshape(-1)

    landing, chosen = plan(sources, devices, per_dev, capacity)
    coef_shape = (nodes,) + node_shape
    payload_shape = pltpu.HBM((slots,) + node_shape, BF16)
    smem = pl.BlockSpec(memory_space=pltpu.SMEM)
    vmem = pl.BlockSpec(memory_space=pltpu.VMEM)
    hbm = pl.BlockSpec(memory_space=pltpu.HBM)

    coef, top_part = pl.pallas_call(
        functools.partial(first_kernel, per_dev),
        in_specs=[hbm, hbm, hbm],
        out_specs=[vmem, vmem],
        out_shape=[pltpu.VMEM(coef_shape, BF16), jax.ShapeDtypeStruct(node_shape, F32)],
        scratch_shapes=[
            pltpu.VMEM(leaf_shape, F32),
            pltpu.VMEM(basis.shape, BF16),
            pltpu.VMEM(transfer.shape, BF16),
            pltpu.SemaphoreType.DMA((2 * per_dev + 1,)),
        ],
        compiler_params=pltpu.CompilerParams(vmem_limit_bytes=60 * MIB),
        cost_estimate=cost(2 * basis.size * classes, 4 * weights.size),
        name="leaf_coefs",
    )(weights3, basis, transfer)
    payload = pl.pallas_call(
        pick_kernel,
        in_specs=[smem, vmem],
        out_specs=hbm,
        out_shape=payload_shape,
        scratch_shapes=[
            pltpu.VMEM(payload_shape.shape, BF16),
            pltpu.SemaphoreType.DMA((8,)),
        ],
        compiler_params=pltpu.CompilerParams(vmem_limit_bytes=60 * MIB),
        cost_estimate=cost(0, 4 * slots * rank_dim * classes),
        name="pick_rows",
    )(chosen, coef)

    def exchange(payload):
        return lax.all_to_all(payload, "leaf", split_axis=0, concat_axis=0, tiled=True)

    halo_shape = (REACH, leaf_size, classes)

    def halo_of(values):
        up = [(i, i + 1) for i in range(devices - 1)]
        down = [(j, i) for i, j in up]
        before = lax.ppermute(values[per_dev - REACH :], "leaf", up)
        after = lax.ppermute(values[:REACH], "leaf", down)
        return before, after

    def near_field(values):
        return pl.pallas_call(
            near_kernel,
            grid=(steps,),
            in_specs=[smem, whole(leaf_shape), per_step(block, near_tiles.shape)],
            out_specs=per_step(block, leaf_shape),
            out_shape=jax.ShapeDtypeStruct(leaf_shape, F32),
            scratch_shapes=[pltpu.VMEM((per_dev + 2 * REACH, leaf_size, classes), BF16)],
            compiler_params=params(16),
            cost_estimate=cost(2 * near_tiles.size * classes, 2 * near_tiles.size),
            name="near_field",
        )(offset_ids, values, near_tiles)

    def with_labels(new):
        return pl.pallas_call(
            shift_kernel,
            grid=(steps,),
            in_specs=[per_step(block, leaf_shape), per_step(block, labels3.shape)],
            out_specs=per_step(block, leaf_shape),
            out_shape=jax.ShapeDtypeStruct(leaf_shape, F32),
            compiler_params=params(16),
            cost_estimate=cost(0, 8 * weights.size),
            name="with_labels",
        )(new, labels3)

    def join(first, second, ahead):
        return pl.pallas_call(
            join_kernel,
            in_specs=[vmem, vmem] + [hbm] * len(ahead),
            out_specs=vmem,
            out_shape=jax.ShapeDtypeStruct((2 * first.shape[0],) + first.shape[1:], BF16),
            compiler_params=pltpu.CompilerParams(vmem_limit_bytes=16 * MIB),
            cost_estimate=cost(0, 4 * first.size),
            name="join_rows",
        )(first, second, *ahead)

    def coarse_rows(top_part, ahead):
        swap = [(i, i ^ 1) for i in range(devices)]
        depth = rank_dim // 2
        core = me & 1
        kept = lax.dynamic_slice_in_dim(top_part, core * depth, depth, axis=0)
        given = lax.dynamic_slice_in_dim(top_part, (1 - core) * depth, depth, axis=0)
        gathered = (kept + lax.ppermute(given, "leaf", swap)).astype(BF16)[None]
        order, hop = [0], 2
        while hop < devices:
            arrived = lax.ppermute(gathered, "leaf", [(i, i ^ hop) for i in range(devices)])
            if 4 * hop == devices:
                gathered = join(gathered, arrived, ahead)
            else:
                gathered = jnp.concatenate([gathered, arrived], axis=0)
            order = order + [place ^ (hop // 2) for place in order]
            hop *= 2
        return order, (gathered, lax.ppermute(gathered, "leaf", swap))

    def finish(incoming, order, halves, near, base, halos, last):
        coarse_levels = devices.bit_length() - 2
        leaf_out = pltpu.HBM(leaf_shape, F32)
        scratch = [
            pltpu.VMEM(payload_shape.shape, BF16),
            pltpu.VMEM(couplings.shape, BF16),
            pltpu.VMEM(transfer.shape, BF16),
            pltpu.VMEM(leaf_shape, F32),
            pltpu.VMEM(leaf_shape, F32),
            pltpu.VMEM(basis.shape, BF16),
            pltpu.VMEM((2 * REACH + 1, leaf_size, classes), BF16),
            pltpu.VMEM((2 * REACH, 2) + near_tiles.shape[2:], BF16),
            pltpu.VMEM(coef_shape, BF16),
            pltpu.VMEM(coef_shape, F32),
            pltpu.VMEM(coarse_transfer.shape, BF16),
            pltpu.VMEM((coarse_levels,) + coarse_couplings.shape[1:], BF16),
            pltpu.VMEM((coarse_couplings.shape[0],) + node_shape, BF16),
        ]
        if last:
            out_shape, out_specs = [leaf_out, leaf_out], [hbm, hbm]
        else:
            out_shape = [
                payload_shape,
                leaf_out,
                pltpu.HBM(leaf_shape, BF16),
                jax.ShapeDtypeStruct(node_shape, F32),
            ]
            out_specs = [hbm, hbm, hbm, vmem]
            scratch += [
                pltpu.VMEM(coef_shape, BF16),
                pltpu.VMEM(payload_shape.shape, BF16),
                pltpu.VMEM(leaf_shape, BF16),
            ]
        scratch.append(pltpu.SemaphoreType.DMA((2 * per_dev + devices,)))
        return pl.pallas_call(
            functools.partial(finish_kernel, devices, order, per_dev, last),
            in_specs=[smem] * 5 + [hbm] * 3 + [vmem] * 2 + [hbm] * 8,
            out_specs=out_specs,
            scratch_shapes=scratch,
            out_shape=out_shape,
            compiler_params=pltpu.CompilerParams(vmem_limit_bytes=60 * MIB),
            cost_estimate=cost(2 * couplings.size * classes, 12 * weights.size),
            name="last_scores" if last else "first_scores",
        )(
            me.reshape(1),
            coarse_sources.reshape(-1),
            landing,
            chosen,
            offset_ids,
            incoming,
            couplings,
            transfer,
            *halves,
            coarse_transfer,
            coarse_couplings,
            near,
            base,
            basis,
            *halos,
            near_tiles,
        )

    labels3 = labels.reshape(per_dev, 1, leaf_size)
    values = weights3.astype(BF16)
    halos = halo_of(values)
    incoming = exchange(payload)
    near = near_field(values)
    base = with_labels(weights3)
    rows = coarse_rows(top_part, (near, base))
    payload, middle, values, top_part = finish(incoming, *rows, near, base, halos, False)
    halos = halo_of(values)
    incoming = exchange(payload)
    near = near_field(values)
    base = with_labels(middle)
    rows = coarse_rows(top_part, (near, base))
    updated, second_scores = finish(incoming, *rows, near, base, halos, True)
    return updated.reshape(weights.shape), second_scores.reshape(weights.shape)


def solution(mesh):
    in_specs = (
        P("leaf", None),
        P("leaf"),
        P("leaf", None, None),
        P("leaf", None, None, None),
        P("leaf", None),
        P("leaf", None, None),
        P("leaf", None, None),
        P("leaf", None),
        P(),
        P(),
        P(),
    )
    out_specs = (P("leaf", None), P("leaf", None))
    return jax.shard_map(local, mesh=mesh, in_specs=in_specs, out_specs=out_specs, check_vma=False)
```

```python
import functools

import jax
import jax.numpy as jnp
import numpy as np
from jax import lax
from jax.experimental import pallas as pl
from jax.experimental.pallas import tpu as pltpu
from jax.sharding import PartitionSpec as P

REACH = 2
STEP_SIZE = 0.5
MIB = 1 << 20
F32 = jnp.float32
BF16 = jnp.bfloat16


def rows_dot(left, right):
    return lax.dot_general(left, right, (((0,), (0,)), ((), ())), preferred_element_type=F32)


def dot(left, right):
    return jnp.dot(left, right, preferred_element_type=F32)


def pair_rows(ref, first):
    both = ref[pl.ds(first, 2)]
    return both.reshape(2 * both.shape[1], both.shape[2])


def tree_rows(per_dev):
    counts = [per_dev >> height for height in range(per_dev.bit_length())]
    starts = [sum(counts[:height]) for height in range(len(counts))]
    return counts, starts


def go_up(coef, transfer, per_dev):
    counts, starts = tree_rows(per_dev)
    for height in range(1, len(counts)):
        for node in range(counts[height]):
            kids = starts[height - 1] + 2 * node
            coef[starts[height] + node] = rows_dot(
                pair_rows(transfer, kids), pair_rows(coef, kids)
            ).astype(BF16)


def go_down(field, coupled, transfer, parent, per_dev):
    counts, starts = tree_rows(per_dev)
    top = starts[-1]
    field[top] = (coupled[top] + dot(transfer[top], parent)).astype(BF16)
    for height in range(len(counts) - 2, -1, -1):
        for node in range(counts[height + 1]):
            kids = starts[height] + 2 * node
            pushed = dot(pair_rows(transfer, kids), field[starts[height + 1] + node])
            both = pair_rows(coupled, kids) + pushed
            field[pl.ds(kids, 2)] = both.reshape(2, -1, both.shape[1]).astype(BF16)


def chunks(total, size):
    return [(low, min(size, total - low)) for low in range(0, total, size)]


class Mover:
    def __init__(self, sems):
        self.sems = sems
        self.used = 0

    def start(self, source, target):
        copy = pltpu.make_async_copy(source, target, self.sems.at[self.used])
        self.used += 1
        copy.start()
        return copy


LEAVES = 8


def first_kernel(per_dev, weights, basis, transfer, coef, top_part, wbuf, bbuf, tbuf, sems):
    mover = Mover(sems)
    parts = chunks(per_dev, LEAVES)
    basis_in = mover.start(basis, bbuf)
    arriving = [mover.start(weights.at[pl.ds(*part)], wbuf.at[pl.ds(*part)]) for part in parts]
    transfer_in = mover.start(transfer, tbuf)
    basis_in.wait()
    for (low, size), copy in zip(parts, arriving):
        copy.wait()
        for leaf in range(low, low + size):
            coef[leaf] = dot(bbuf[leaf], wbuf[leaf].astype(BF16)).astype(BF16)
    transfer_in.wait()
    go_up(coef, tbuf, per_dev)
    top = coef.shape[0] - 1
    top_part[...] = rows_dot(tbuf[top], coef[top])


def pick(mover, chosen, coef, buffer, payload):
    leaving = []
    total = payload.shape[0]
    for low, size in chunks(total, max(total // 2, 1)):
        for slot in range(low, low + size):
            buffer[slot] = coef[chosen(slot)]
        rows = pl.ds(low, size)
        leaving.append(mover.start(buffer.at[rows], payload.at[rows]))
    return leaving


def pick_kernel(chosen, coef, payload, buffer, sems):
    width = chosen.shape[2]
    for copy in pick(
        Mover(sems), lambda slot: chosen[slot // width, 0, slot % width], coef, buffer, payload
    ):
        copy.wait()


def near_kernel(ids, own, tiles, out, padded):
    step = pl.program_id(0)
    block = tiles.shape[0]
    inner = own.shape[0]

    @pl.when(step == 0)
    def _():
        nothing = jnp.zeros((REACH,) + own.shape[1:], BF16)
        padded[pl.ds(0, REACH)] = nothing
        padded[pl.ds(REACH, inner)] = own[...]
        padded[pl.ds(REACH + inner, REACH)] = nothing

    for leaf in range(block):
        row = step * block + leaf
        out[leaf] = (
            dot(tiles[leaf, 0], padded[row + REACH])
            + dot(tiles[leaf, 1], padded[ids[2 * row]])
            + dot(tiles[leaf, 2], padded[ids[2 * row + 1]])
        ).astype(out.dtype)


def join_kernel(first, second, *rest):
    joined = rest[-1]
    size = first.shape[0]
    joined[pl.ds(0, size)] = first[...]
    joined[pl.ds(size, size)] = second[...]


def edge_scores(ids, leaf, tiles, halo, per_dev):
    total = None
    for member in range(2):
        row = ids(2 * leaf + member)
        place = jnp.where(row < REACH, row, jnp.where(row < REACH + per_dev, 2 * REACH, row - per_dev))
        term = dot(tiles[member], halo[place])
        total = term if total is None else total + term
    return total


def coarse_parent(devices, order, mine, listed, halves, transfer, couplings, coef):
    levels = devices.bit_length() - 2
    links = couplings.shape[2] // couplings.shape[1]
    offsets = [devices - (devices >> level - 1) for level in range(1, levels + 1)]
    depth = halves[0].shape[1]
    for turn, half in enumerate(halves):
        rows = pl.ds(pl.multiple_of(jnp.bitwise_xor(mine & 1, turn) * depth, depth), depth)
        for place in range(devices // 2):
            coef[jnp.bitwise_xor(mine >> 1, order[place]), rows] = half[place]
    for level in range(1, levels):
        for node in range(devices >> level + 1):
            kids = offsets[level - 1] + 2 * node
            coef[offsets[level] + node] = rows_dot(
                pair_rows(transfer, kids), pair_rows(coef, kids)
            ).astype(BF16)
    field = None
    for level in range(levels, 0, -1):
        offset = offsets[level - 1]
        node = offset + (mine >> level)
        blocks = jnp.concatenate(
            [coef[offset + listed(node * links + link)] for link in range(links)], axis=0
        )
        term = dot(couplings[level - 1], blocks)
        if level < levels:
            term = term + dot(transfer[node], field)
        field = term.astype(BF16)
    return field


def finish_kernel(
    devices,
    order,
    per_dev,
    last,
    table,
    incoming,
    couplings,
    transfer,
    half,
    other_half,
    coarse_transfer,
    coarse_couplings,
    near,
    base,
    basis,
    before,
    after,
    tiles,
    *rest,
):
    if last:
        new_out, scores_out = rest[:2]
        rest = rest[2:]
        scores_buf = rest[-2]
    else:
        payload, grads_out, top_part = rest[:3]
        rest = rest[3:]
        coef, buffer, grads = rest[-4:-1]
    inbuf, cbuf, tbuf, nbuf, abuf, bbuf, halo, edge_tiles, field, coupled = rest[:10]
    coarse_maps, coarse_mats, coarse_coef = rest[10:13]
    sems = rest[-1]
    nodes = couplings.shape[0]
    links = couplings.shape[2] // couplings.shape[1]
    mine = table[0]
    places = {}
    used = 1
    for name, size in (
        ("listed", coarse_couplings.shape[0] * links),
        ("landing", (nodes + 1) * links),
        ("chosen", incoming.shape[0]),
        ("ids", 2 * per_dev),
    ):
        places[name] = used
        used += size

    def entry(name, place):
        return table[places[name] + place]

    mover = Mover(sems)
    low_edge, high_edge = pl.ds(0, REACH), pl.ds(per_dev - REACH, REACH)
    others = pl.ds(1, 2)
    coarse_in = [mover.start(coarse_transfer, coarse_maps)]
    for level in range(1, coarse_mats.shape[0] + 1):
        node = devices - (devices >> level - 1) + (mine >> level)
        coarse_in.append(mover.start(coarse_couplings.at[node], coarse_mats.at[level - 1]))
    blocks_in, mats_in, maps_in, *edges_in = [
        mover.start(*pair)
        for pair in (
            (incoming, inbuf),
            (couplings, cbuf),
            (transfer, tbuf),
            (basis, bbuf),
            (before, halo.at[pl.ds(0, REACH)]),
            (after, halo.at[pl.ds(REACH, REACH)]),
            (tiles.at[low_edge, others], edge_tiles.at[pl.ds(0, REACH)]),
            (tiles.at[high_edge, others], edge_tiles.at[pl.ds(REACH, REACH)]),
        )
    ]
    leaves_in = [
        [
            mover.start(source.at[pl.ds(*part)], target.at[pl.ds(*part)])
            for source, target in ((near, nbuf), (base, abuf))
        ]
        for part in chunks(per_dev, LEAVES)
    ]
    halo[2 * REACH] = jnp.zeros(halo.shape[1:], BF16)
    for copy in coarse_in:
        copy.wait()
    parent = coarse_parent(
        devices, order, mine, functools.partial(entry, "listed"), (half, other_half), coarse_maps, coarse_mats, coarse_coef
    )
    blocks_in.wait()
    mats_in.wait()
    for node in range(nodes - 1, -1, -1):
        blocks = jnp.concatenate(
            [inbuf[entry("landing", link * (nodes + 1) + node)] for link in range(links)], axis=0
        )
        coupled[node] = dot(cbuf[node], blocks)
    maps_in.wait()
    go_down(field, coupled, tbuf, parent, per_dev)
    leaving = []
    for copy in edges_in:
        copy.wait()
    for (low, size), copies in zip(chunks(per_dev, LEAVES), leaves_in):
        for copy in copies:
            copy.wait()
        rows = pl.ds(low, size)
        for leaf in range(low, low + size):
            scores = nbuf[leaf].astype(F32) + rows_dot(bbuf[leaf], field[leaf])
            edge = leaf if leaf < REACH else leaf - (per_dev - 2 * REACH)
            if leaf < REACH or leaf >= per_dev - REACH:
                scores = scores + edge_scores(
                    functools.partial(entry, "ids"), leaf, edge_tiles.at[edge], halo, per_dev
                )
            step = gradient(scores)
            new = abuf[leaf] - step
            if last:
                scores_buf[leaf] = scores
                abuf[leaf] = new
            else:
                grads[leaf] = step.astype(BF16)
                coef[leaf] = dot(bbuf[leaf], new.astype(BF16)).astype(BF16)
        if last:
            leaving.append(mover.start(scores_buf.at[rows], scores_out.at[rows]))
            leaving.append(mover.start(abuf.at[rows], new_out.at[rows]))
    if not last:
        go_up(coef, tbuf, per_dev)
        leaving += pick(mover, functools.partial(entry, "chosen"), coef, buffer, payload)
        leaving.append(mover.start(grads, grads_out))
        top_part[...] = rows_dot(tbuf[nodes - 1], coef[nodes - 1])
    for copy in leaving:
        copy.wait()


def gradient(scores):
    return (0.5 * STEP_SIZE) * (1.0 + jnp.tanh(0.5 * scores))


def shifted(new, labels, classes):
    marks = lax.broadcasted_iota(jnp.int32, (classes, labels.shape[1]), 0) == labels
    eye = lax.broadcasted_iota(jnp.int32, (classes, classes), 0) == lax.broadcasted_iota(
        jnp.int32, (classes, classes), 1
    )
    return new + STEP_SIZE * rows_dot(marks.astype(BF16), eye.astype(BF16))


def step_kernel(old, grads, labels, base, values):
    for leaf in range(old.shape[0]):
        new = old[leaf] - grads[leaf].astype(F32)
        values[leaf] = new.astype(BF16)
        base[leaf] = shifted(new, labels[leaf], new.shape[1])


def shift_kernel(new, labels, base):
    for leaf in range(new.shape[0]):
        base[leaf] = shifted(new[leaf], labels[leaf], new.shape[2])


def whole(shape):
    return pl.BlockSpec(shape, lambda i, *_: (0,) * len(shape), pipeline_mode=pl.Buffered(1))


def whole_out(shape):
    return pl.BlockSpec(shape, lambda i, *_: (0,) * len(shape))


def per_step(block, shape):
    return pl.BlockSpec((block,) + tuple(shape[1:]), lambda i, *_: (i,) + (0,) * (len(shape) - 1))


def params(limit):
    return pltpu.CompilerParams(
        dimension_semantics=("arbitrary",), vmem_limit_bytes=limit * MIB
    )


def cost(flops, moved):
    return pl.CostEstimate(flops=int(flops), bytes_accessed=int(moved), transcendentals=0)


def plan_kernel(per_dev, capacity, sources, landing, wanted):
    links, nodes = sources.shape
    devices = wanted.shape[0]
    counts, starts = tree_rows(per_dev)
    padded = nodes + 1
    width = links * padded
    node = lax.broadcasted_iota(jnp.int32, (links, padded), 1)
    shift = jnp.zeros_like(node)
    start = jnp.zeros_like(node)
    for height, first in enumerate(starts):
        shift = jnp.where(node >= first, len(counts) - 1 - height, shift)
        start = jnp.where(node >= first, first, start)
    listed = jnp.concatenate([sources[...], jnp.zeros((links, 1), jnp.int32)], axis=1)
    owner = jnp.where(node < nodes, listed >> shift, -1)
    row = start + (listed & ((1 << shift) - 1))

    def in_line(values):
        return jnp.concatenate([values[link : link + 1] for link in range(links)], axis=1)

    rows_along = in_line(row)
    along = jnp.broadcast_to(in_line(owner), (width, width))
    down = along.T
    later = lax.broadcasted_iota(jnp.int32, (width, width), 0) < lax.broadcasted_iota(
        jnp.int32, (width, width), 1
    )
    rank = jnp.sum(jnp.where((down == along) & later, 1.0, 0.0), axis=0, keepdims=True)
    rank = rank.astype(jnp.int32)
    landing[...] = along[:1] * capacity + rank
    device = lax.broadcasted_iota(jnp.int32, (devices, width), 0)
    named = jnp.where(device == along[:1], rows_along.astype(F32), 0.0)
    wanted[:, 0, :] = jnp.concatenate(
        [
            jnp.sum(jnp.where(rank == place, named, 0.0), axis=1, keepdims=True)
            for place in range(capacity)
        ],
        axis=1,
    ).astype(jnp.int32)


def plan(sources, devices, per_dev, capacity):
    nodes, links = sources.shape
    landing, wanted = pl.pallas_call(
        functools.partial(plan_kernel, per_dev, capacity),
        out_shape=[
            jax.ShapeDtypeStruct((1, links * (nodes + 1)), jnp.int32),
            jax.ShapeDtypeStruct((devices, 1, capacity), jnp.int32),
        ],
        name="plan",
    )(sources.T)
    chosen = lax.all_to_all(wanted, "leaf", split_axis=0, concat_axis=0, tiled=True)
    return landing.reshape(-1), chosen


def local(
    weights,
    labels,
    basis,
    near_tiles,
    near_ids,
    transfer,
    couplings,
    sources,
    coarse_transfer,
    coarse_couplings,
    coarse_sources,
):
    devices = lax.axis_size("leaf")
    me = lax.axis_index("leaf")
    per_dev, rank_dim, leaf_size = basis.shape
    classes = weights.shape[1]
    nodes = transfer.shape[0]
    links = sources.shape[1]
    capacity = nodes * links // devices + 1
    slots = devices * capacity
    block = next(size for size in (4, 2, 1) if per_dev % size == 0)
    steps = per_dev // block
    node_shape = (rank_dim, classes)
    leaf_shape = (per_dev, leaf_size, classes)
    weights3 = weights.reshape(leaf_shape)
    offset_ids = (near_ids - (me * per_dev - REACH)).reshape(-1)

    landing, chosen = plan(sources, devices, per_dev, capacity)
    coef_shape = (nodes,) + node_shape
    payload_shape = pltpu.HBM((slots,) + node_shape, BF16)
    smem = pl.BlockSpec(memory_space=pltpu.SMEM)
    vmem = pl.BlockSpec(memory_space=pltpu.VMEM)
    hbm = pl.BlockSpec(memory_space=pltpu.HBM)

    far = functools.partial(pltpu.with_memory_space_constraint, memory_space=pltpu.HBM)
    coef, top_part = pl.pallas_call(
        functools.partial(first_kernel, per_dev),
        in_specs=[hbm, hbm, hbm],
        out_specs=[vmem, vmem],
        out_shape=[pltpu.VMEM(coef_shape, BF16), jax.ShapeDtypeStruct(node_shape, F32)],
        scratch_shapes=[
            pltpu.VMEM(leaf_shape, F32),
            pltpu.VMEM(basis.shape, BF16),
            pltpu.VMEM(transfer.shape, BF16),
            pltpu.SemaphoreType.DMA((2 * per_dev + 1,)),
        ],
        compiler_params=pltpu.CompilerParams(vmem_limit_bytes=20 * MIB),
        cost_estimate=cost(2 * basis.size * classes, 4 * weights.size),
        name="leaf_coefs",
    )(*[far(value) for value in (weights3, basis, transfer)])
    payload = pl.pallas_call(
        pick_kernel,
        in_specs=[smem, vmem],
        out_specs=hbm,
        out_shape=payload_shape,
        scratch_shapes=[
            pltpu.VMEM(payload_shape.shape, BF16),
            pltpu.SemaphoreType.DMA((8,)),
        ],
        compiler_params=pltpu.CompilerParams(vmem_limit_bytes=20 * MIB),
        cost_estimate=cost(0, 4 * slots * rank_dim * classes),
        name="pick_rows",
    )(chosen, coef)

    def exchange(payload):
        return lax.all_to_all(payload, "leaf", split_axis=0, concat_axis=0, tiled=True)

    halo_shape = (REACH, leaf_size, classes)

    def halo_of(values):
        up = [(i, i + 1) for i in range(devices - 1)]
        down = [(j, i) for i, j in up]
        before = lax.ppermute(values[per_dev - REACH :], "leaf", up)
        after = lax.ppermute(values[:REACH], "leaf", down)
        return before, after

    def near_field(values):
        return pl.pallas_call(
            near_kernel,
            grid=(steps,),
            in_specs=[smem, whole(leaf_shape), per_step(block, near_tiles.shape)],
            out_specs=per_step(block, leaf_shape),
            out_shape=jax.ShapeDtypeStruct(leaf_shape, BF16),
            scratch_shapes=[pltpu.VMEM((per_dev + 2 * REACH, leaf_size, classes), BF16)],
            compiler_params=params(16),
            cost_estimate=cost(2 * near_tiles.size * classes, 2 * near_tiles.size),
            name="near_field",
        )(offset_ids, values, near_tiles)

    labels3 = labels.reshape(per_dev, 1, leaf_size)
    part = per_step(block, leaf_shape)
    label_part = per_step(block, labels3.shape)

    def with_labels(new):
        return pl.pallas_call(
            shift_kernel,
            grid=(steps,),
            in_specs=[part, label_part],
            out_specs=part,
            out_shape=jax.ShapeDtypeStruct(leaf_shape, F32),
            compiler_params=params(16),
            cost_estimate=cost(0, 8 * weights.size),
            name="with_labels",
        )(new, labels3)

    def step_with_labels(old, grads):
        return pl.pallas_call(
            step_kernel,
            grid=(steps,),
            in_specs=[part, part, label_part],
            out_specs=[part, part],
            out_shape=[
                jax.ShapeDtypeStruct(leaf_shape, F32),
                jax.ShapeDtypeStruct(leaf_shape, BF16),
            ],
            compiler_params=params(16),
            cost_estimate=cost(0, 12 * weights.size),
            name="step_with_labels",
        )(old, grads, labels3)

    def join(first, second, ahead):
        return pl.pallas_call(
            join_kernel,
            in_specs=[vmem, vmem] + [hbm] * len(ahead),
            out_specs=vmem,
            out_shape=jax.ShapeDtypeStruct((2 * first.shape[0],) + first.shape[1:], BF16),
            compiler_params=pltpu.CompilerParams(vmem_limit_bytes=16 * MIB),
            cost_estimate=cost(0, 4 * first.size),
            name="join_rows",
        )(first, second, *ahead)

    def coarse_rows(top_part, ahead):
        swap = [(i, i ^ 1) for i in range(devices)]
        depth = rank_dim // 2
        core = me & 1
        kept = lax.dynamic_slice_in_dim(top_part, core * depth, depth, axis=0)
        given = lax.dynamic_slice_in_dim(top_part, (1 - core) * depth, depth, axis=0)
        gathered = (kept + lax.ppermute(given, "leaf", swap)).astype(BF16)[None]
        order, hop = [0], 2
        while hop < devices:
            arrived = lax.ppermute(gathered, "leaf", [(i, i ^ hop) for i in range(devices)])
            if 4 * hop == devices:
                gathered = join(gathered, arrived, ahead)
            else:
                gathered = jnp.concatenate([gathered, arrived], axis=0)
            order = order + [place ^ (hop // 2) for place in order]
            hop *= 2
        return order, (gathered, lax.ppermute(gathered, "leaf", swap))

    def finish(incoming, order, halves, near, base, halos, last):
        coarse_levels = devices.bit_length() - 2
        leaf_out = pltpu.HBM(leaf_shape, F32)
        scratch = [
            pltpu.VMEM(payload_shape.shape, BF16),
            pltpu.VMEM(couplings.shape, BF16),
            pltpu.VMEM(transfer.shape, BF16),
            pltpu.VMEM(leaf_shape, BF16),
            pltpu.VMEM(leaf_shape, F32),
            pltpu.VMEM(basis.shape, BF16),
            pltpu.VMEM((2 * REACH + 1, leaf_size, classes), BF16),
            pltpu.VMEM((2 * REACH, 2) + near_tiles.shape[2:], BF16),
            pltpu.VMEM(coef_shape, BF16),
            pltpu.VMEM(coef_shape, F32),
            pltpu.VMEM(coarse_transfer.shape, BF16),
            pltpu.VMEM((coarse_levels,) + coarse_couplings.shape[1:], BF16),
            pltpu.VMEM((coarse_couplings.shape[0],) + node_shape, BF16),
        ]
        if last:
            out_shape, out_specs = [leaf_out, leaf_out], [hbm, hbm]
            scratch.append(pltpu.VMEM(leaf_shape, F32))
        else:
            out_shape = [
                payload_shape,
                pltpu.HBM(leaf_shape, BF16),
                jax.ShapeDtypeStruct(node_shape, F32),
            ]
            out_specs = [hbm, hbm, vmem]
            scratch += [
                pltpu.VMEM(coef_shape, BF16),
                pltpu.VMEM(payload_shape.shape, BF16),
                pltpu.VMEM(leaf_shape, BF16),
            ]
        scratch.append(pltpu.SemaphoreType.DMA((2 * per_dev + devices,)))
        return pl.pallas_call(
            functools.partial(finish_kernel, devices, order, per_dev, last),
            in_specs=[smem] + [hbm] * 3 + [vmem] * 2 + [hbm] * 8,
            out_specs=out_specs,
            scratch_shapes=scratch,
            out_shape=out_shape,
            compiler_params=pltpu.CompilerParams(vmem_limit_bytes=40 * MIB),
            cost_estimate=cost(2 * couplings.size * classes, 12 * weights.size),
            name="last_scores" if last else "first_scores",
        )(
            table,
            far(incoming),
            far(couplings),
            far(transfer),
            *halves,
            far(coarse_transfer),
            far(coarse_couplings),
            far(near),
            far(base),
            far(basis),
            *[far(halo) for halo in halos],
            far(near_tiles),
        )

    table = jnp.concatenate(
        [me.reshape(1), coarse_sources.reshape(-1), landing, chosen.reshape(-1), offset_ids]
    )
    values = weights3.astype(BF16)
    halos = halo_of(values)
    incoming = exchange(payload)
    near = near_field(values)
    base = with_labels(weights3)
    rows = coarse_rows(top_part, (near, base, table))
    payload, grads, top_part = finish(incoming, *rows, near, base, halos, False)
    incoming = exchange(payload)
    base, values = step_with_labels(base, grads)
    halos = halo_of(values)
    near = near_field(values)
    rows = coarse_rows(top_part, (near, base, table))
    updated, second_scores = finish(incoming, *rows, near, base, halos, True)
    return updated.reshape(weights.shape), second_scores.reshape(weights.shape)


def solution(mesh):
    in_specs = (
        P("leaf", None),
        P("leaf"),
        P("leaf", None, None),
        P("leaf", None, None, None),
        P("leaf", None),
        P("leaf", None, None),
        P("leaf", None, None),
        P("leaf", None),
        P(),
        P(),
        P(),
    )
    out_specs = (P("leaf", None), P("leaf", None))
    return jax.shard_map(local, mesh=mesh, in_specs=in_specs, out_specs=out_specs, check_vma=False)
```

```python
import functools

import jax
import jax.numpy as jnp
import numpy as np
from jax import lax
from jax.experimental import pallas as pl
from jax.experimental.pallas import tpu as pltpu
from jax.sharding import PartitionSpec as P

REACH = 2
STEP_SIZE = 0.5
MIB = 1 << 20
F32 = jnp.float32
BF16 = jnp.bfloat16


def rows_dot(left, right):
    return lax.dot_general(left, right, (((0,), (0,)), ((), ())), preferred_element_type=F32)


def dot(left, right):
    return jnp.dot(left, right, preferred_element_type=F32)


def pair_rows(ref, first):
    both = ref[pl.ds(first, 2)]
    return both.reshape(2 * both.shape[1], both.shape[2])


def tree_rows(per_dev):
    counts = [per_dev >> height for height in range(per_dev.bit_length())]
    starts = [sum(counts[:height]) for height in range(len(counts))]
    return counts, starts


def go_up(coef, transfer, per_dev):
    counts, starts = tree_rows(per_dev)
    for height in range(1, len(counts)):
        for node in range(counts[height]):
            kids = starts[height - 1] + 2 * node
            coef[starts[height] + node] = rows_dot(
                pair_rows(transfer, kids), pair_rows(coef, kids)
            ).astype(BF16)


def go_up_from(leaf, coef, transfer, per_dev):
    counts, starts = tree_rows(per_dev)
    for height in range(1, len(counts)):
        if (leaf + 1) % (1 << height):
            break
        kids = starts[height - 1] + 2 * (leaf >> height)
        coef[starts[height] + (leaf >> height)] = rows_dot(
            pair_rows(transfer, kids), pair_rows(coef, kids)
        ).astype(BF16)


def go_down(field, coupled, transfer, parent, per_dev):
    counts, starts = tree_rows(per_dev)
    top = starts[-1]
    field[top] = (coupled[top] + dot(transfer[top], parent)).astype(BF16)
    for height in range(len(counts) - 2, -1, -1):
        for node in range(counts[height + 1]):
            kids = starts[height] + 2 * node
            pushed = dot(pair_rows(transfer, kids), field[starts[height + 1] + node])
            both = pair_rows(coupled, kids) + pushed
            field[pl.ds(kids, 2)] = both.reshape(2, -1, both.shape[1]).astype(BF16)


def chunks(total, size):
    return [(low, min(size, total - low)) for low in range(0, total, size)]


class Mover:
    def __init__(self, sems):
        self.sems = sems
        self.used = 0

    def start(self, source, target):
        copy = pltpu.make_async_copy(source, target, self.sems.at[self.used])
        self.used += 1
        copy.start()
        return copy


LEAVES = 8


def first_kernel(per_dev, weights, basis, transfer, coef, top_part, wbuf, bbuf, tbuf, sems):
    mover = Mover(sems)
    parts = chunks(per_dev, LEAVES)
    basis_in = mover.start(basis, bbuf)
    arriving = [mover.start(weights.at[pl.ds(*part)], wbuf.at[pl.ds(*part)]) for part in parts]
    transfer_in = mover.start(transfer, tbuf)
    basis_in.wait()
    for (low, size), copy in zip(parts, arriving):
        copy.wait()
        for leaf in range(low, low + size):
            coef[leaf] = dot(bbuf[leaf], wbuf[leaf].astype(BF16)).astype(BF16)
    transfer_in.wait()
    go_up(coef, tbuf, per_dev)
    top = coef.shape[0] - 1
    top_part[...] = rows_dot(tbuf[top], coef[top])


def pick(mover, chosen, coef, buffer, payload):
    leaving = []
    total = payload.shape[0]
    for low, size in chunks(total, max(total // 4, 1)):
        for slot in range(low, low + size):
            buffer[slot] = coef[chosen(slot)]
        rows = pl.ds(low, size)
        leaving.append(mover.start(buffer.at[rows], payload.at[rows]))
    return leaving


def pick_kernel(chosen, coef, payload, buffer, sems):
    width = chosen.shape[2]
    for copy in pick(
        Mover(sems), lambda slot: chosen[slot // width, 0, slot % width], coef, buffer, payload
    ):
        copy.wait()


def near_kernel(ids, own, tiles, out, padded):
    step = pl.program_id(0)
    block = tiles.shape[0]
    inner = own.shape[0]

    @pl.when(step == 0)
    def _():
        nothing = jnp.zeros((REACH,) + own.shape[1:], BF16)
        padded[pl.ds(0, REACH)] = nothing
        padded[pl.ds(REACH, inner)] = own[...]
        padded[pl.ds(REACH + inner, REACH)] = nothing

    for leaf in range(block):
        row = step * block + leaf
        out[leaf] = (
            dot(tiles[leaf, 0], padded[row + REACH])
            + dot(tiles[leaf, 1], padded[ids[2 * row]])
            + dot(tiles[leaf, 2], padded[ids[2 * row + 1]])
        ).astype(out.dtype)


def join_kernel(first, second, *rest):
    joined = rest[-1]
    size = first.shape[0]
    joined[pl.ds(0, size)] = first[...]
    joined[pl.ds(size, size)] = second[...]


def edge_scores(ids, leaf, tiles, halo, per_dev):
    total = None
    for member in range(2):
        row = ids(2 * leaf + member)
        place = jnp.where(row < REACH, row, jnp.where(row < REACH + per_dev, 2 * REACH, row - per_dev))
        term = dot(tiles[member], halo[place])
        total = term if total is None else total + term
    return total


def coarse_parent(devices, order, mine, listed, halves, transfer, couplings, coef):
    levels = devices.bit_length() - 2
    links = couplings.shape[2] // couplings.shape[1]
    offsets = [devices - (devices >> level - 1) for level in range(1, levels + 1)]
    depth = halves[0].shape[1]
    for turn, half in enumerate(halves):
        rows = pl.ds(pl.multiple_of(jnp.bitwise_xor(mine & 1, turn) * depth, depth), depth)
        for place in range(devices // 2):
            coef[jnp.bitwise_xor(mine >> 1, order[place]), rows] = half[place]
    for level in range(1, levels):
        for node in range(devices >> level + 1):
            kids = offsets[level - 1] + 2 * node
            coef[offsets[level] + node] = rows_dot(
                pair_rows(transfer, kids), pair_rows(coef, kids)
            ).astype(BF16)
    field = None
    for level in range(levels, 0, -1):
        offset = offsets[level - 1]
        node = offset + (mine >> level)
        blocks = jnp.concatenate(
            [coef[offset + listed(node * links + link)] for link in range(links)], axis=0
        )
        term = dot(couplings[level - 1], blocks)
        if level < levels:
            term = term + dot(transfer[node], field)
        field = term.astype(BF16)
    return field


def finish_kernel(
    devices,
    order,
    per_dev,
    last,
    table,
    incoming,
    couplings,
    transfer,
    half,
    other_half,
    coarse_transfer,
    coarse_couplings,
    near,
    base,
    basis,
    before,
    after,
    tiles,
    *rest,
):
    if last:
        new_out, scores_out = rest[:2]
        rest = rest[2:]
        scores_buf = rest[-2]
    else:
        payload, grads_out, top_part = rest[:3]
        rest = rest[3:]
        coef, buffer, grads = rest[-4:-1]
    inbuf, cbuf, tbuf, nbuf, abuf, bbuf, halo, edge_tiles, field, coupled = rest[:10]
    coarse_maps, coarse_mats, coarse_coef = rest[10:13]
    sems = rest[-1]
    nodes = couplings.shape[0]
    links = couplings.shape[2] // couplings.shape[1]
    mine = table[0]
    places = {}
    used = 1
    for name, size in (
        ("listed", coarse_couplings.shape[0] * links),
        ("landing", (nodes + 1) * links),
        ("chosen", incoming.shape[0]),
        ("ids", 2 * per_dev),
    ):
        places[name] = used
        used += size

    def entry(name, place):
        return table[places[name] + place]

    mover = Mover(sems)
    low_edge, high_edge = pl.ds(0, REACH), pl.ds(per_dev - REACH, REACH)
    others = pl.ds(1, 2)
    coarse_in = [mover.start(coarse_transfer, coarse_maps)]
    for level in range(1, coarse_mats.shape[0] + 1):
        node = devices - (devices >> level - 1) + (mine >> level)
        coarse_in.append(mover.start(coarse_couplings.at[node], coarse_mats.at[level - 1]))
    blocks_in, mats_in, maps_in, *edges_in = [
        mover.start(*pair)
        for pair in (
            (incoming, inbuf),
            (couplings, cbuf),
            (transfer, tbuf),
            (basis, bbuf),
            (before, halo.at[pl.ds(0, REACH)]),
            (after, halo.at[pl.ds(REACH, REACH)]),
            (tiles.at[low_edge, others], edge_tiles.at[pl.ds(0, REACH)]),
            (tiles.at[high_edge, others], edge_tiles.at[pl.ds(REACH, REACH)]),
        )
    ]
    leaves_in = [
        [
            mover.start(source.at[pl.ds(*part)], target.at[pl.ds(*part)])
            for source, target in ((near, nbuf), (base, abuf))
        ]
        for part in chunks(per_dev, LEAVES)
    ]
    halo[2 * REACH] = jnp.zeros(halo.shape[1:], BF16)
    for copy in coarse_in:
        copy.wait()
    parent = coarse_parent(
        devices, order, mine, functools.partial(entry, "listed"), (half, other_half), coarse_maps, coarse_mats, coarse_coef
    )
    blocks_in.wait()
    mats_in.wait()
    for node in range(nodes - 1, -1, -1):
        blocks = jnp.concatenate(
            [inbuf[entry("landing", link * (nodes + 1) + node)] for link in range(links)], axis=0
        )
        coupled[node] = dot(cbuf[node], blocks)
    maps_in.wait()
    go_down(field, coupled, tbuf, parent, per_dev)
    leaving = []
    for copy in edges_in:
        copy.wait()
    for (low, size), copies in zip(chunks(per_dev, LEAVES), leaves_in):
        for copy in copies:
            copy.wait()
        rows = pl.ds(low, size)
        for leaf in range(low, low + size):
            scores = nbuf[leaf].astype(F32) + rows_dot(bbuf[leaf], field[leaf])
            edge = leaf if leaf < REACH else leaf - (per_dev - 2 * REACH)
            if leaf < REACH or leaf >= per_dev - REACH:
                scores = scores + edge_scores(
                    functools.partial(entry, "ids"), leaf, edge_tiles.at[edge], halo, per_dev
                )
            step = gradient(scores)
            new = abuf[leaf] - step
            if last:
                scores_buf[leaf] = scores
                abuf[leaf] = new
            else:
                grads[leaf] = step.astype(BF16)
                coef[leaf] = dot(bbuf[leaf], new.astype(BF16)).astype(BF16)
                go_up_from(leaf, coef, tbuf, per_dev)
        if last:
            leaving.append(mover.start(scores_buf.at[rows], scores_out.at[rows]))
            leaving.append(mover.start(abuf.at[rows], new_out.at[rows]))
    if not last:
        leaving += pick(mover, functools.partial(entry, "chosen"), coef, buffer, payload)
        leaving.append(mover.start(grads, grads_out))
        top_part[...] = rows_dot(tbuf[nodes - 1], coef[nodes - 1])
    for copy in leaving:
        copy.wait()


def gradient(scores):
    return (0.5 * STEP_SIZE) * (1.0 + jnp.tanh(0.5 * scores))


def shifted(new, labels, classes):
    marks = lax.broadcasted_iota(jnp.int32, (classes, labels.shape[1]), 0) == labels
    eye = lax.broadcasted_iota(jnp.int32, (classes, classes), 0) == lax.broadcasted_iota(
        jnp.int32, (classes, classes), 1
    )
    return new + STEP_SIZE * rows_dot(marks.astype(BF16), eye.astype(BF16))


def step_kernel(old, grads, labels, base, values):
    for leaf in range(old.shape[0]):
        new = old[leaf] - grads[leaf].astype(F32)
        values[leaf] = new.astype(BF16)
        base[leaf] = shifted(new, labels[leaf], new.shape[1])


def shift_kernel(new, labels, base):
    for leaf in range(new.shape[0]):
        base[leaf] = shifted(new[leaf], labels[leaf], new.shape[2])


def whole(shape):
    return pl.BlockSpec(shape, lambda i, *_: (0,) * len(shape), pipeline_mode=pl.Buffered(1))


def whole_out(shape):
    return pl.BlockSpec(shape, lambda i, *_: (0,) * len(shape))


def per_step(block, shape):
    return pl.BlockSpec((block,) + tuple(shape[1:]), lambda i, *_: (i,) + (0,) * (len(shape) - 1))


def params(limit):
    return pltpu.CompilerParams(
        dimension_semantics=("arbitrary",), vmem_limit_bytes=limit * MIB
    )


def cost(flops, moved):
    return pl.CostEstimate(flops=int(flops), bytes_accessed=int(moved), transcendentals=0)


def plan_kernel(per_dev, capacity, sources, landing, wanted):
    links, nodes = sources.shape
    devices = wanted.shape[0]
    counts, starts = tree_rows(per_dev)
    padded = nodes + 1
    width = links * padded
    node = lax.broadcasted_iota(jnp.int32, (links, padded), 1)
    shift = jnp.zeros_like(node)
    start = jnp.zeros_like(node)
    for height, first in enumerate(starts):
        shift = jnp.where(node >= first, len(counts) - 1 - height, shift)
        start = jnp.where(node >= first, first, start)
    listed = jnp.concatenate([sources[...], jnp.zeros((links, 1), jnp.int32)], axis=1)
    owner = jnp.where(node < nodes, listed >> shift, -1)
    row = start + (listed & ((1 << shift) - 1))

    def in_line(values):
        return jnp.concatenate([values[link : link + 1] for link in range(links)], axis=1)

    rows_along = in_line(row)
    along = jnp.broadcast_to(in_line(owner), (width, width))
    down = along.T
    later = lax.broadcasted_iota(jnp.int32, (width, width), 0) < lax.broadcasted_iota(
        jnp.int32, (width, width), 1
    )
    rank = jnp.sum(jnp.where((down == along) & later, 1.0, 0.0), axis=0, keepdims=True)
    rank = rank.astype(jnp.int32)
    landing[...] = along[:1] * capacity + rank
    device = lax.broadcasted_iota(jnp.int32, (devices, width), 0)
    named = jnp.where(device == along[:1], rows_along.astype(F32), 0.0)
    wanted[:, 0, :] = jnp.concatenate(
        [
            jnp.sum(jnp.where(rank == place, named, 0.0), axis=1, keepdims=True)
            for place in range(capacity)
        ],
        axis=1,
    ).astype(jnp.int32)


def plan(sources, devices, per_dev, capacity):
    nodes, links = sources.shape
    landing, wanted = pl.pallas_call(
        functools.partial(plan_kernel, per_dev, capacity),
        out_shape=[
            jax.ShapeDtypeStruct((1, links * (nodes + 1)), jnp.int32),
            jax.ShapeDtypeStruct((devices, 1, capacity), jnp.int32),
        ],
        name="plan",
    )(sources.T)
    chosen = lax.all_to_all(wanted, "leaf", split_axis=0, concat_axis=0, tiled=True)
    return landing.reshape(-1), chosen


def local(
    weights,
    labels,
    basis,
    near_tiles,
    near_ids,
    transfer,
    couplings,
    sources,
    coarse_transfer,
    coarse_couplings,
    coarse_sources,
):
    devices = lax.axis_size("leaf")
    me = lax.axis_index("leaf")
    per_dev, rank_dim, leaf_size = basis.shape
    classes = weights.shape[1]
    nodes = transfer.shape[0]
    links = sources.shape[1]
    capacity = nodes * links // devices + 1
    slots = devices * capacity
    block = next(size for size in (4, 2, 1) if per_dev % size == 0)
    steps = per_dev // block
    node_shape = (rank_dim, classes)
    leaf_shape = (per_dev, leaf_size, classes)
    weights3 = weights.reshape(leaf_shape)
    offset_ids = (near_ids - (me * per_dev - REACH)).reshape(-1)

    landing, chosen = plan(sources, devices, per_dev, capacity)
    coef_shape = (nodes,) + node_shape
    payload_shape = pltpu.HBM((slots,) + node_shape, BF16)
    smem = pl.BlockSpec(memory_space=pltpu.SMEM)
    vmem = pl.BlockSpec(memory_space=pltpu.VMEM)
    hbm = pl.BlockSpec(memory_space=pltpu.HBM)

    far = functools.partial(pltpu.with_memory_space_constraint, memory_space=pltpu.HBM)
    coef, top_part = pl.pallas_call(
        functools.partial(first_kernel, per_dev),
        in_specs=[hbm, hbm, hbm],
        out_specs=[vmem, vmem],
        out_shape=[pltpu.VMEM(coef_shape, BF16), jax.ShapeDtypeStruct(node_shape, F32)],
        scratch_shapes=[
            pltpu.VMEM(leaf_shape, F32),
            pltpu.VMEM(basis.shape, BF16),
            pltpu.VMEM(transfer.shape, BF16),
            pltpu.SemaphoreType.DMA((2 * per_dev + 1,)),
        ],
        compiler_params=pltpu.CompilerParams(vmem_limit_bytes=20 * MIB),
        cost_estimate=cost(2 * basis.size * classes, 4 * weights.size),
        name="leaf_coefs",
    )(*[far(value) for value in (weights3, basis, transfer)])
    payload = pl.pallas_call(
        pick_kernel,
        in_specs=[smem, vmem],
        out_specs=hbm,
        out_shape=payload_shape,
        scratch_shapes=[
            pltpu.VMEM(payload_shape.shape, BF16),
            pltpu.SemaphoreType.DMA((8,)),
        ],
        compiler_params=pltpu.CompilerParams(vmem_limit_bytes=20 * MIB),
        cost_estimate=cost(0, 4 * slots * rank_dim * classes),
        name="pick_rows",
    )(chosen, coef)

    def exchange(payload):
        return lax.all_to_all(payload, "leaf", split_axis=0, concat_axis=0, tiled=True)

    halo_shape = (REACH, leaf_size, classes)

    def halo_of(values):
        up = [(i, i + 1) for i in range(devices - 1)]
        down = [(j, i) for i, j in up]
        before = lax.ppermute(values[per_dev - REACH :], "leaf", up)
        after = lax.ppermute(values[:REACH], "leaf", down)
        return before, after

    def near_field(values):
        return pl.pallas_call(
            near_kernel,
            grid=(steps,),
            in_specs=[smem, whole(leaf_shape), per_step(block, near_tiles.shape)],
            out_specs=per_step(block, leaf_shape),
            out_shape=jax.ShapeDtypeStruct(leaf_shape, BF16),
            scratch_shapes=[pltpu.VMEM((per_dev + 2 * REACH, leaf_size, classes), BF16)],
            compiler_params=params(16),
            cost_estimate=cost(2 * near_tiles.size * classes, 2 * near_tiles.size),
            name="near_field",
        )(offset_ids, values, near_tiles)

    labels3 = labels.reshape(per_dev, 1, leaf_size)
    part = per_step(block, leaf_shape)
    label_part = per_step(block, labels3.shape)

    def with_labels(new):
        return pl.pallas_call(
            shift_kernel,
            grid=(steps,),
            in_specs=[part, label_part],
            out_specs=part,
            out_shape=jax.ShapeDtypeStruct(leaf_shape, F32),
            compiler_params=params(16),
            cost_estimate=cost(0, 8 * weights.size),
            name="with_labels",
        )(new, labels3)

    def step_with_labels(old, grads):
        return pl.pallas_call(
            step_kernel,
            grid=(steps,),
            in_specs=[part, part, label_part],
            out_specs=[part, part],
            out_shape=[
                jax.ShapeDtypeStruct(leaf_shape, F32),
                jax.ShapeDtypeStruct(leaf_shape, BF16),
            ],
            compiler_params=params(16),
            cost_estimate=cost(0, 12 * weights.size),
            name="step_with_labels",
        )(old, grads, labels3)

    def join(first, second, ahead):
        return pl.pallas_call(
            join_kernel,
            in_specs=[vmem, vmem] + [hbm] * len(ahead),
            out_specs=vmem,
            out_shape=jax.ShapeDtypeStruct((2 * first.shape[0],) + first.shape[1:], BF16),
            compiler_params=pltpu.CompilerParams(vmem_limit_bytes=16 * MIB),
            cost_estimate=cost(0, 4 * first.size),
            name="join_rows",
        )(first, second, *ahead)

    def coarse_rows(top_part, ahead):
        swap = [(i, i ^ 1) for i in range(devices)]
        depth = rank_dim // 2
        core = me & 1
        kept = lax.dynamic_slice_in_dim(top_part, core * depth, depth, axis=0)
        given = lax.dynamic_slice_in_dim(top_part, (1 - core) * depth, depth, axis=0)
        gathered = (kept + lax.ppermute(given, "leaf", swap)).astype(BF16)[None]
        order, hop = [0], 2
        while hop < devices:
            arrived = lax.ppermute(gathered, "leaf", [(i, i ^ hop) for i in range(devices)])
            if 4 * hop == devices:
                gathered = join(gathered, arrived, ahead)
            else:
                gathered = jnp.concatenate([gathered, arrived], axis=0)
            order = order + [place ^ (hop // 2) for place in order]
            hop *= 2
        return order, (gathered, lax.ppermute(gathered, "leaf", swap))

    def finish(incoming, order, halves, near, base, halos, last):
        coarse_levels = devices.bit_length() - 2
        leaf_out = pltpu.HBM(leaf_shape, F32)
        scratch = [
            pltpu.VMEM(payload_shape.shape, BF16),
            pltpu.VMEM(couplings.shape, BF16),
            pltpu.VMEM(transfer.shape, BF16),
            pltpu.VMEM(leaf_shape, BF16),
            pltpu.VMEM(leaf_shape, F32),
            pltpu.VMEM(basis.shape, BF16),
            pltpu.VMEM((2 * REACH + 1, leaf_size, classes), BF16),
            pltpu.VMEM((2 * REACH, 2) + near_tiles.shape[2:], BF16),
            pltpu.VMEM(coef_shape, BF16),
            pltpu.VMEM(coef_shape, F32),
            pltpu.VMEM(coarse_transfer.shape, BF16),
            pltpu.VMEM((coarse_levels,) + coarse_couplings.shape[1:], BF16),
            pltpu.VMEM((coarse_couplings.shape[0],) + node_shape, BF16),
        ]
        if last:
            out_shape, out_specs = [leaf_out, leaf_out], [hbm, hbm]
            scratch.append(pltpu.VMEM(leaf_shape, F32))
        else:
            out_shape = [
                payload_shape,
                pltpu.HBM(leaf_shape, BF16),
                jax.ShapeDtypeStruct(node_shape, F32),
            ]
            out_specs = [hbm, hbm, vmem]
            scratch += [
                pltpu.VMEM(coef_shape, BF16),
                pltpu.VMEM(payload_shape.shape, BF16),
                pltpu.VMEM(leaf_shape, BF16),
            ]
        scratch.append(pltpu.SemaphoreType.DMA((2 * per_dev + devices,)))
        return pl.pallas_call(
            functools.partial(finish_kernel, devices, order, per_dev, last),
            in_specs=[smem] + [hbm] * 3 + [vmem] * 2 + [hbm] * 8,
            out_specs=out_specs,
            scratch_shapes=scratch,
            out_shape=out_shape,
            compiler_params=pltpu.CompilerParams(vmem_limit_bytes=40 * MIB),
            cost_estimate=cost(2 * couplings.size * classes, 12 * weights.size),
            name="last_scores" if last else "first_scores",
        )(
            table,
            far(incoming),
            far(couplings),
            far(transfer),
            *halves,
            far(coarse_transfer),
            far(coarse_couplings),
            far(near),
            far(base),
            far(basis),
            *[far(halo) for halo in halos],
            far(near_tiles),
        )

    table = jnp.concatenate(
        [me.reshape(1), coarse_sources.reshape(-1), landing, chosen.reshape(-1), offset_ids]
    )
    values = weights3.astype(BF16)
    halos = halo_of(values)
    incoming = exchange(payload)
    near = near_field(values)
    base = with_labels(weights3)
    rows = coarse_rows(top_part, (near, base, table))
    payload, grads, top_part = finish(incoming, *rows, near, base, halos, False)
    incoming = exchange(payload)
    base, values = step_with_labels(base, grads)
    halos = halo_of(values)
    near = near_field(values)
    rows = coarse_rows(top_part, (near, base, table))
    updated, second_scores = finish(incoming, *rows, near, base, halos, True)
    return updated.reshape(weights.shape), second_scores.reshape(weights.shape)


def solution(mesh):
    in_specs = (
        P("leaf", None),
        P("leaf"),
        P("leaf", None, None),
        P("leaf", None, None, None),
        P("leaf", None),
        P("leaf", None, None),
        P("leaf", None, None),
        P("leaf", None),
        P(),
        P(),
        P(),
    )
    out_specs = (P("leaf", None), P("leaf", None))
    return jax.shard_map(local, mesh=mesh, in_specs=in_specs, out_specs=out_specs, check_vma=False)
```
